512 devices in a mesh: dp: 64 (over y, z), tensor: 8 (over x, core).
Axes of the slice: x: 4, y: 4, z: 16, core: 2. Of those that a mesh axis runs over, the one named last changes fastest.
Arguments:
- queries: bfloat16 [24576, 8192], P(('dp', 'tensor'))
- keys: bfloat16 [24576, 1024], P(('dp', 'tensor')), may hold values from -5 to 5
- values: bfloat16 [24576, 1024], P(('dp', 'tensor')), may hold values from -12 to 12
- ancestors: int32 [256, 6], P('dp'), may hold values from -1 to 255, as said below
Outputs:
- attended: bfloat16 [24576, 8192], P(('dp', 'tensor'))
The draws below stay inside these ranges and needn't reach their ends.
Inputs may be any that keep to these rules, and one draw needn't show every extreme that they name: Block b consists of tokens b * 96 to (b + 1) * 96 - 1 and lies on dp index b // 4; its family is b % 2 and its copy (b // 2) % 2. Each row lists the chain of ancestors of its block, nearest first (entry k + 1 is the parent of entry k), then -1 in the remaining entries. Ancestors have the block's family and copy and lie on a dp index that differs from the block's by a multiple of 4, at most (15) * 4 away, and with the same remainder modulo 4; those of family 0 lie at lower dp indices, those of family 1 at higher ones. In every tree some block lists 6 ancestors.
All inputs are finite; a program needn't handle non-finite values.
Results may differ from the reference program's by a relative error of at most 0.0032.
Values may be sent and summed in bfloat16 or wider, within the bound.
A program may use at most 64 MiB of HBM per device.

```python
import math
import jax
import jax.numpy as jnp
from jax import lax

HEADS = 64
KVH = 8
HD = 128
NODE = 96
TG = 16
ANC = 6
BLOCKS = 256
TOKENS = 24576


def normal_keys(key):
    sample = jax.random.normal(key, (TOKENS, KVH * HD), jnp.float32)
    return jnp.clip(sample, -5.0, 5.0)


def draw_keys(key, part):
    base_table = normal_keys(key)
    return base_table.astype(jnp.bfloat16)


def draw_queries(key, part):
    key = jax.random.fold_in(key, 12)
    sample = 2.0 * jnp.clip(jax.random.normal(key, (TOKENS, HEADS * HD), jnp.float32), -5.0, 5.0)
    return sample.astype(jnp.bfloat16)


def block_of(tree_pos, family_ids, copy_ids, group_index):
    spacing = BLOCKS // (4 * TG)
    device = group_index + spacing * jnp.where(family_ids == 0, tree_pos, TG - 1 - tree_pos)
    return (device * 4 + copy_ids * 2 + family_ids).astype(jnp.int32)


def draw_ancestors(key, part):
    key = jax.random.fold_in(key, 13)
    tree_count = BLOCKS // TG
    columns = jnp.arange(TG, dtype=jnp.int32)

    def extend(position, tree_state):
        parents, depths = tree_state
        scores = jax.random.randint(jax.random.fold_in(key, position), (tree_count, TG), 0, 4096, dtype=jnp.int32) * TG + columns[None, :]
        allowed = (columns[None, :] < position) & (depths < ANC)
        chosen = jnp.argmax(jnp.where(allowed, scores, -1), axis=1).astype(jnp.int32)
        chosen = jnp.where(position <= ANC, position - 1, chosen).astype(jnp.int32)
        depth_new = jnp.take_along_axis(depths, chosen[:, None], axis=1)[:, 0] + 1
        parents = parents.at[:, position].set(chosen)
        depths = depths.at[:, position].set(depth_new)
        return (parents, depths)
    start_state = (jnp.full((tree_count, TG), -1, jnp.int32), jnp.zeros((tree_count, TG), jnp.int32))
    parents, depths = lax.fori_loop(1, TG, extend, start_state)
    chain_list = []
    current = parents
    for depth_level in range(ANC):
        chain_list.append(current)
        current = jnp.where(current >= 0, jnp.take_along_axis(parents, jnp.maximum(current, 0), axis=1), -1)
    chain_table = jnp.stack(chain_list, axis=2)
    tree_ids = jnp.arange(tree_count, dtype=jnp.int32)[:, None]
    family_ids = tree_ids % 2
    copy_ids = tree_ids // 2 % 2
    group_ids = tree_ids // 4
    own_ids = block_of(columns[None, :], family_ids, copy_ids, group_ids)
    listed = jnp.where(chain_table >= 0, block_of(chain_table, family_ids[:, :, None], copy_ids[:, :, None], group_ids[:, :, None]), -1)
    ancestor_table = jnp.zeros((BLOCKS, ANC), jnp.int32).at[own_ids.reshape(-1)].set(listed.reshape(-1, ANC).astype(jnp.int32))
    return ancestor_table


def level_of(rng, extent, pieces, low, top_value):
    gain, own = 1.0, jax.random.fold_in(rng, 6)
    for axis_at, blocks in pieces:
        heights = jnp.exp(jax.random.uniform(jax.random.fold_in(own, axis_at), (blocks,), jnp.float32, low / len(pieces), top_value / len(pieces)))
        gain = gain * jnp.repeat(heights, extent[axis_at] // blocks).reshape([-1 if axis == axis_at else 1 for axis in range(len(extent))])
    return gain


def noise(rng, shape, spread, bound, pieces=(), kind=jnp.bfloat16):
    factor_of = level_of(rng, shape, pieces, -0.22, 0.18) if pieces else 1.0
    result = jax.random.normal(rng, shape, jnp.float32) * spread * factor_of
    return jnp.minimum(jnp.maximum(result, -bound), bound).astype(kind)


def setup_inputs(seed: int = 0) -> dict:
    arg_keys = jax.random.split(jax.random.key(seed), 5)
    return {
        "queries": draw_queries(jax.random.fold_in(arg_keys[4], 71), 0),
        "keys": draw_keys(jax.random.fold_in(arg_keys[4], 71), 0),
        "values": noise(arg_keys[2], (TOKENS, KVH * HD), 2.0, 12.0, ((0, 512),)),
        "ancestors": draw_ancestors(jax.random.fold_in(arg_keys[4], 71), 0),
    }


def block_mask(listed, block_rows):
    listed_live = jnp.repeat(listed >= 0, block_rows)
    row_ids = jnp.arange(block_rows, dtype=jnp.int32)
    causal = row_ids[None, :] <= row_ids[:, None]
    spread_live = jnp.broadcast_to(listed_live[None, :], (block_rows, listed_live.shape[0]))
    return jnp.concatenate([spread_live, causal], axis=1)

def attend_rows(queries_blk, key_rows, value_rows, visible):
    scores = jnp.einsum('qkgd,lkd->kgql', queries_blk, key_rows) * (1.0 / math.sqrt(HD))
    masked = jnp.where(visible, scores, -1e+30)
    row_max = lax.optimization_barrier(jnp.max(masked, axis=-1, keepdims=True))
    weights = jnp.where(visible, jnp.exp(masked - row_max), 0.0)
    weight_sum = lax.optimization_barrier(jnp.sum(weights, axis=-1))
    rounded = lax.optimization_barrier(weights.astype(jnp.bfloat16)).astype(jnp.float32)
    combined = jnp.einsum('kgql,lkd->qkgd', rounded, value_rows)
    return (combined / jnp.transpose(weight_sum, (2, 0, 1))[..., None]).astype(jnp.bfloat16)

def reference(queries, keys, values, ancestors):
    group_size = HEADS // KVH
    query_blocks = queries.reshape(BLOCKS, NODE, KVH, group_size, HD)
    key_blocks = keys.reshape(BLOCKS, NODE, KVH, HD)
    value_blocks = values.reshape(BLOCKS, NODE, KVH, HD)

    def attend_block(block_index):
        listed = ancestors[block_index]
        picked = jnp.clip(listed, 0, BLOCKS - 1).astype(jnp.int32)
        key_rows = jnp.concatenate([key_blocks[picked].reshape(ANC * NODE, KVH, HD), key_blocks[block_index]], axis=0).astype(jnp.float32)
        value_rows = jnp.concatenate([value_blocks[picked].reshape(ANC * NODE, KVH, HD), value_blocks[block_index]], axis=0).astype(jnp.float32)
        visible = block_mask(listed, NODE)
        return attend_rows(query_blocks[block_index].astype(jnp.float32), key_rows, value_rows, visible)
    attended = lax.map(attend_block, jnp.arange(BLOCKS, dtype=jnp.int32))
    return attended.reshape(TOKENS, HEADS * HD)
```

```python
import functools
import math

import jax
import jax.numpy as jnp
from jax import lax
from jax.experimental import pallas as pl
from jax.experimental.pallas import tpu as pltpu
from jax.sharding import PartitionSpec as P

HD = 128
NODE = 96
HALF = 48
ANC = 6
KEYS = (ANC + 1) * NODE
GROUP = 8
HEADS = 4
JOINT = 4
MESH = pl.DeviceIdType.MESH
EXP_SCALE = math.log2(math.e) / math.sqrt(HD)


def kernel(q_ref, k_ref, v_ref, anc_ref, out_ref, kv0, kv1, kv2, kv3, q_s, o_s, bias_s,
           own_l, own_s, own_r, q_sem, zs, zf, zr, zo, ys, yr, os_, or_, ol):
    kv = (kv0, kv1, kv2, kv3)
    dp, t = lax.axis_index("dp"), lax.axis_index("tensor")
    x, c = t // 2, t % 2
    y, w, g = dp // 16, (dp % 16) // 4, dp % 4
    f = x % 2
    Y = y + f * (3 - 2 * y)
    W = w + f * (3 - 2 * w)

    def dev(row, col):
        yy = row + f * (3 - 2 * row)
        ww = col + f * (3 - 2 * col)
        return (yy * 16 + ww * 4 + g, t)

    cols = [lax.rem(W + i, 4) for i in range(4)]
    me = Y * 4 + W
    sibling = (dp, x * 2 + 1 - c)
    z_next, z_prev = dev(Y, cols[1]), dev(Y, cols[3])
    y_next, y_prev = dev(lax.rem(Y + 1, 4), W), dev(lax.rem(Y + 3, 4), W)
    mine = pl.ds(pl.multiple_of(c * HALF, 16), HALF)
    theirs = pl.ds(pl.multiple_of((1 - c) * HALF, 16), HALF)

    def lanes(start, size):
        return pl.ds(pl.multiple_of(start, 128), size)

    own = []
    for h in range(HEADS):
        for i, ref in enumerate((k_ref, v_ref)):
            n = h * 2 + i
            local = pltpu.make_async_copy(
                ref.at[:, lanes(c * 512 + h * HD, HD)], kv[h].at[me, i, mine], own_l.at[n])
            remote = pltpu.make_async_remote_copy(
                ref.at[:, lanes((1 - c) * 512 + h * HD, HD)], kv[h].at[me, i, mine],
                own_s.at[n], own_r.at[n], device_id=sibling, device_id_type=MESH)
            local.start()
            own.append((local, remote))
    q_local = pltpu.make_async_copy(q_ref.at[:, lanes(c * 4096, 4096)], q_s.at[mine], q_sem.at[0])
    q_remote = pltpu.make_async_remote_copy(
        q_ref.at[:, lanes((1 - c) * 4096, 4096)], q_s.at[mine], q_sem.at[1], q_sem.at[2],
        device_id=sibling, device_id_type=MESH)
    q_local.start()

    barrier = pltpu.get_barrier_semaphore()
    for partner in (sibling, z_next, z_prev, y_next, y_prev):
        pl.semaphore_signal(barrier, inc=1, device_id=partner, device_id_type=MESH)
    pl.semaphore_wait(barrier, 5)

    for _, remote in own:
        remote.start()
    q_remote.start()

    sent = []

    def send(src, dst, s_sem, r_sem, to, when=None):
        copy = pltpu.make_async_remote_copy(src, dst, s_sem, r_sem, device_id=to, device_id_type=MESH)
        if when is None:
            copy.start()
        else:
            pl.when(when)(copy.start)
        sent.append((copy, when))

    def arrived(ref, sem, when=None):
        copy = pltpu.make_async_remote_copy(ref, ref, sem, sem, device_id=sibling, device_id_type=MESH)
        if when is None:
            copy.wait_recv()
        else:
            pl.when(when)(copy.wait_recv)

    def y_block(h, row, i, to, n, when):
        slot = row * 4 + cols[i]
        send(kv[h].at[slot], kv[h].at[slot], ys.at[h, n], yr.at[h, slot], to, when)

    def y_own(h, i):
        y_block(h, Y, i, y_next, i, Y < 3)
        if i % 2 == 0:
            y_block(h, Y, i, y_prev, 4 + i, Y == 0)
        else:
            y_block(h, Y, i, y_prev, 4 + i, Y < 2)

    def y_arrived(h, row, i, when):
        slot = row * 4 + cols[i]
        arrived(kv[h].at[slot], yr.at[h, slot], when)

    def send_own(h):
        for i in range(2):
            local, remote = own[h * 2 + i]
            local.wait()
            remote.wait_recv()
        src = kv[h].at[me]
        send(src, src, zs.at[h, 0], zr.at[h, 0], z_next)
        send(src, src, zs.at[h, 1], zr.at[h, 1], z_prev)
        y_own(h, 0)

    def z_near(h):
        for n, i, to in ((0, 3, z_next), (1, 1, z_prev)):
            slot = kv[h].at[Y * 4 + cols[i]]
            arrived(slot, zr.at[h, n])
            send(slot.at[n], slot.at[n], zf.at[h, n], zo.at[h, n], to)
            y_own(h, i)

    def z_far(h):
        slot = kv[h].at[Y * 4 + cols[2]]
        for n in range(2):
            arrived(slot.at[n], zo.at[h, n])
        y_own(h, 2)

    def relay(h, i):
        if i % 2 == 0:
            y_arrived(h, 1, i, Y == 2)
            y_block(h, 1, i, y_next, 8 + i, Y == 2)
        else:
            y_arrived(h, 1, i, Y == 0)
            y_block(h, 1, i, y_prev, 8 + i, Y == 0)
        y_arrived(h, 0, i, Y == 3)
        y_block(h, 0, i, y_prev, 8 + i, Y == 3)

    def rest(h):
        for i in range(4):
            y_arrived(h, 0, i, Y == 1)
            if i % 2 == 1:
                y_arrived(h, 1, i, Y == 2)
            y_arrived(h, 0, i, Y == 2)
            y_arrived(h, 2, i, Y == 3)
            y_arrived(h, 1, i, Y == 3)

    listed = [anc_ref[x, i] for i in range(ANC)]
    places = []
    for a in listed:
        a0 = jnp.maximum(a, 0)
        ay, aw = a0 >> 6, (a0 >> 4) & 3
        ay = ay + f * (3 - 2 * ay)
        aw = aw + f * (3 - 2 * aw)
        places.append(jnp.where(a >= 0, ay * 4 + aw, me))
    places.append(me)

    def build_bias():
        rows = lax.broadcasted_iota(jnp.int32, (NODE, KEYS), 0)
        at = lax.broadcasted_iota(jnp.int32, (NODE, KEYS), 1)
        bias = jnp.where(at - ANC * NODE > rows, -1e30, 0.0)
        for i, a in enumerate(listed):
            inside = (at >= NODE * i) & (at < NODE * (i + 1))
            bias = jnp.where(inside, jnp.where(a >= 0, 0.0, -1e30), bias)
        bias_s[...] = bias

    out_copies = []

    def attend(h):
        keys = jnp.concatenate([kv[h][s, 0] for s in places], axis=0)
        values = jnp.concatenate([kv[h][s, 1] for s in places], axis=0)
        for first in range(0, GROUP, JOINT):
            at = [(h * GROUP + first + j) * HD for j in range(JOINT)]
            queries = jnp.concatenate([q_s[:, a:a + HD] for a in at], axis=0)
            scores = lax.dot_general(queries, keys, (((1,), (1,)), ((), ())), preferred_element_type=jnp.float32)
            scores = (scores.reshape(JOINT, NODE, KEYS) + bias_s[...][None]).reshape(JOINT * NODE, KEYS)
            top = jnp.max(scores, axis=-1, keepdims=True)
            weights = jnp.exp2((scores - top) * EXP_SCALE)
            total = jnp.sum(weights, axis=-1, keepdims=True)
            mixed = jnp.dot(weights.astype(jnp.bfloat16), values, preferred_element_type=jnp.float32)
            mixed = (mixed / total).astype(jnp.bfloat16)
            for j in range(JOINT):
                o_s[:, at[j]:at[j] + HD] = mixed[j * NODE:(j + 1) * NODE]
        width = GROUP * HD
        there = out_ref.at[:, lanes(c * 4096 + h * width, width)]
        local = pltpu.make_async_copy(o_s.at[mine, pl.ds(h * width, width)], there, ol.at[h])
        remote = pltpu.make_async_remote_copy(
            o_s.at[theirs, pl.ds(h * width, width)], there, os_.at[h], or_.at[h],
            device_id=sibling, device_id_type=MESH)
        local.start()
        remote.start()
        out_copies.append((local, remote))

    def relays(h):
        for i in (0, 3, 1, 2):
            relay(h, i)

    send_own(0)
    send_own(1)
    build_bias()
    q_local.wait()
    q_remote.wait_recv()
    z_near(0)
    send_own(2)
    z_near(1)
    z_far(0)
    send_own(3)
    relays(0)
    z_near(2)
    z_far(1)
    rest(0)
    attend(0)
    relays(1)
    z_near(3)
    z_far(2)
    rest(1)
    attend(1)
    relays(2)
    z_far(3)
    rest(2)
    attend(2)
    relays(3)
    rest(3)
    attend(3)

    for _, remote in own:
        remote.wait_send()
    q_remote.wait_send()
    for copy, when in sent:
        if when is None:
            copy.wait_send()
        else:
            pl.when(when)(copy.wait_send)
    for local, remote in out_copies:
        local.wait()
        remote.wait()


def local(queries, keys, values, ancestors):
    kv = pltpu.VMEM((16, 2, NODE, HD), jnp.bfloat16)
    dma = pltpu.SemaphoreType.DMA
    anywhere = pl.BlockSpec(memory_space=pl.ANY)
    return pl.pallas_call(
        kernel,
        out_shape=jax.ShapeDtypeStruct((HALF, 8192), jnp.bfloat16),
        in_specs=[anywhere, anywhere, anywhere, pl.BlockSpec(memory_space=pltpu.SMEM)],
        out_specs=anywhere,
        scratch_shapes=[
            kv, kv, kv, kv,
            pltpu.VMEM((NODE, 4096), jnp.bfloat16),
            pltpu.VMEM((NODE, 4096), jnp.bfloat16),
            pltpu.VMEM((NODE, KEYS), jnp.float32),
            dma((8,)), dma((8,)), dma((8,)), dma((3,)),
            dma((4, 2)), dma((4, 2)), dma((4, 2)), dma((4, 2)),
            dma((4, 12)), dma((4, 16)),
            dma((4,)), dma((4,)), dma((4,)),
        ],
        compiler_params=pltpu.CompilerParams(
            collective_id=0, has_side_effects=True, vmem_limit_bytes=48 << 20),
        cost_estimate=pl.CostEstimate(flops=2 * 2 * 96 * 32 * 672 * 128, bytes_accessed=4 << 20, transcendentals=96 * 32 * 672),
        name="tree_attention",
    )(queries, keys, values, ancestors)


def solution(mesh):
    split = P(("dp", "tensor"), None)
    return jax.shard_map(
        local, mesh=mesh, in_specs=(split, split, split, P("dp", None)), out_specs=split, check_vma=False)
```

```python
import math

import jax
import jax.numpy as jnp
from jax import lax
from jax.experimental import pallas as pl
from jax.experimental.pallas import tpu as pltpu
from jax.sharding import PartitionSpec as P

HD = 128
NODE = 96
HALF = 48
ANC = 6
KEYS = (ANC + 1) * NODE
GROUP = 8
JOINT = 4
MESH = pl.DeviceIdType.MESH
EXP_SCALE = math.log2(math.e) / math.sqrt(HD)
UNITS = ((0, 0), (1, 0), (1, 1), (0, 1))


def kernel(q_ref, k_ref, v_ref, anc_hbm, out_ref, anc_ref, anc_sem, kv0, kv1, kv2, kv3, q_s, o_s, bias_s,
           kv_l, kv_s, kv_r, q_l, q_t, q_r, zs, zf, zr, zo, ys, yr, o_l, o_t, o_r):
    kv = (kv0, kv1, kv2, kv3)
    dp, t = lax.axis_index("dp"), lax.axis_index("tensor")
    x, c = t // 2, t % 2
    y, w, g = dp // 16, (dp % 16) // 4, dp % 4
    px = x + 1 - 2 * (x % 2)
    r = t % 4

    fam = [x % 2, px % 2]
    rows = [y + f * (3 - 2 * y) for f in fam]
    cols = [w + f * (3 - 2 * w) for f in fam]
    me = [rows[b] * 4 + cols[b] for b in range(2)]

    def dev(b, row, col):
        yy = row + fam[b] * (3 - 2 * row)
        ww = col + fam[b] * (3 - 2 * col)
        return (yy * 16 + ww * 4 + g, t)

    def col_at(b, i):
        return lax.rem(cols[b] + i, 4)

    sibling = (dp, x * 2 + 1 - c)
    across = [(dp, px * 2 + cc) for cc in range(2)]
    mine = pl.ds(pl.multiple_of(c * HALF, 16), HALF)
    theirs = pl.ds(pl.multiple_of((1 - c) * HALF, 16), HALF)

    def lanes(start, size):
        return pl.ds(pl.multiple_of(start, 128), size)

    def remote(src, dst, s_sem, r_sem, to):
        return pltpu.make_async_remote_copy(src, dst, s_sem, r_sem, device_id=to, device_id_type=MESH)

    sent = []

    def send(src, dst, s_sem, r_sem, to, when=None):
        copy = remote(src, dst, s_sem, r_sem, to)
        if when is None:
            copy.start()
        else:
            pl.when(when)(copy.start)
        sent.append((copy, when))

    def drain():
        for copy, when in sent:
            if when is None:
                copy.wait_send()
            else:
                pl.when(when)(copy.wait_send)
        sent.clear()

    def arrived(ref, sem, when=None):
        copy = remote(ref, ref, sem, sem, sibling)
        if when is None:
            copy.wait_recv()
        else:
            pl.when(when)(copy.wait_recv)

    anc_copy = pltpu.make_async_copy(anc_hbm, anc_ref, anc_sem)
    anc_copy.start()
    kv_local = {}
    for u in (0, 3):
        i = UNITS[u][1]
        for n, ref in enumerate((k_ref, v_ref)):
            copy = pltpu.make_async_copy(
                ref.at[:, lanes((r * 2 + i) * HD, HD)], kv[u].at[me[0], n, mine], kv_l.at[i, n])
            copy.start()
            kv_local[u, n] = copy
    q_local = pltpu.make_async_copy(q_ref.at[:, lanes(r * 2048, 2048)], q_s.at[0, mine], q_l.at[0])
    q_local.start()

    barrier = pltpu.get_barrier_semaphore()
    others = [dev(0, rows[0], col_at(0, 1)), dev(0, rows[0], col_at(0, 3))]
    others += [dev(0, lax.rem(rows[0] + d, 4), cols[0]) for d in (2, 1, 3)] + [*across, sibling]
    for partner in others:
        pl.semaphore_signal(barrier, inc=1, device_id=partner, device_id_type=MESH)
    pl.semaphore_wait(barrier, len(others))

    def share(u):
        b, i = UNITS[u]
        for n, ref in enumerate((k_ref, v_ref)):
            if b == 0:
                rr = x % 2 * 2 + 1 - c
                send(ref.at[:, lanes((rr * 2 + i) * HD, HD)], kv[u].at[me[0], n, mine],
                     kv_s.at[u, n, 0], kv_r.at[u, n, 0], sibling)
            else:
                for cc in range(2):
                    rr = px % 2 * 2 + cc
                    send(ref.at[:, lanes((rr * 2 + i) * HD, HD)], kv[u].at[me[0], n, mine],
                         kv_s.at[u, n, cc], kv_r.at[u, n, c], across[cc])

    def share_queries():
        for cc in range(2):
            rr = px % 2 * 2 + cc
            send(q_ref.at[:, lanes(rr * 2048, 2048)], q_s.at[1, mine], q_t.at[cc], q_r.at[c], across[cc])
        rr = x % 2 * 2 + 1 - c
        send(q_ref.at[:, lanes(rr * 2048, 2048)], q_s.at[0, mine], q_t.at[2], q_r.at[2], sibling)

    def own_ready(u):
        b, i = UNITS[u]
        for n in range(2):
            if b == 0:
                kv_local[u, n].wait()
                arrived(kv[u].at[me[0], n, theirs], kv_r.at[u, n, 0])
            else:
                for cc in range(2):
                    arrived(kv[u].at[me[1], n, pl.ds(cc * HALF, HALF)], kv_r.at[u, n, cc])

    def y_send(u, i):
        b = UNITS[u][0]
        block = kv[u].at[rows[b] * 4 + col_at(b, i)]
        for d in (1, 2, 3):
            send(block, block, ys.at[u, i, d - 1], yr.at[u, rows[b] * 4 + col_at(b, i)],
                 dev(b, lax.rem(rows[b] + d, 4), cols[b]), rows[b] + d < 4)

    def send_own(u):
        own_ready(u)
        b = UNITS[u][0]
        block = kv[u].at[me[b]]
        send(block, block, zs.at[u, 0], zr.at[u, 0], dev(b, rows[b], col_at(b, 1)))
        send(block, block, zs.at[u, 1], zr.at[u, 1], dev(b, rows[b], col_at(b, 3)))

    def z_near(u):
        b = UNITS[u][0]
        for n, i, to in ((0, 3, 1), (1, 1, 3)):
            block = kv[u].at[rows[b] * 4 + col_at(b, i)]
            arrived(block, zr.at[u, n])
            send(block.at[n], block.at[n], zf.at[u, n], zo.at[u, n], dev(b, rows[b], col_at(b, to)))
            y_send(u, i)

    def z_far(u):
        b = UNITS[u][0]
        block = kv[u].at[rows[b] * 4 + col_at(b, 2)]
        for n in range(2):
            arrived(block.at[n], zo.at[u, n])
        y_send(u, 2)

    def rest(u):
        b = UNITS[u][0]
        for row in range(3):
            for i in (0, 3, 1, 2):
                slot = row * 4 + col_at(b, i)
                arrived(kv[u].at[slot], yr.at[u, slot], rows[b] > row)

    places, listed = [], []

    def read_ancestors():
        anc_copy.wait()
        listed.extend([[anc_ref[x if b == 0 else px, i] for i in range(ANC)] for b in range(2)])
        for b in range(2):
            found = []
            for a in listed[b]:
                a0 = jnp.maximum(a, 0)
                ay, aw = a0 >> 6, (a0 >> 4) & 3
                ay = ay + fam[b] * (3 - 2 * ay)
                aw = aw + fam[b] * (3 - 2 * aw)
                found.append(jnp.where(a >= 0, ay * 4 + aw, me[b]))
            places.append(found + [me[b]])

    def build_bias():
        at_row = lax.broadcasted_iota(jnp.int32, (NODE, KEYS), 0)
        at = lax.broadcasted_iota(jnp.int32, (NODE, KEYS), 1)
        causal = jnp.where(at - ANC * NODE > at_row, -1e30, 0.0)
        for b in range(2):
            bias = causal
            for i, a in enumerate(listed[b]):
                inside = (at >= NODE * i) & (at < NODE * (i + 1))
                bias = jnp.where(inside, jnp.where(a >= 0, 0.0, -1e30), bias)
            bias_s[b] = bias

    out_copies = []

    def attend(u):
        b, i = UNITS[u]
        keys = jnp.concatenate([kv[u][s, 0] for s in places[b]], axis=0)
        values = jnp.concatenate([kv[u][s, 1] for s in places[b]], axis=0)
        for first in range(0, GROUP, JOINT):
            at = [(i * GROUP + first + j) * HD for j in range(JOINT)]
            queries = jnp.concatenate([q_s[b, :, a:a + HD] for a in at], axis=0)
            scores = lax.dot_general(queries, keys, (((1,), (1,)), ((), ())), preferred_element_type=jnp.float32)
            scores = (scores.reshape(JOINT, NODE, KEYS) + bias_s[b][None]).reshape(JOINT * NODE, KEYS)
            top = jnp.max(scores, axis=-1, keepdims=True)
            weights = jnp.exp2((scores - top) * EXP_SCALE)
            total = jnp.sum(weights, axis=-1, keepdims=True)
            mixed = jnp.dot(weights.astype(jnp.bfloat16), values, preferred_element_type=jnp.float32)
            mixed = (mixed / total).astype(jnp.bfloat16)
            for j in range(JOINT):
                o_s[u, :, (first + j) * HD:(first + j + 1) * HD] = mixed[j * NODE:(j + 1) * NODE]
        there = out_ref.at[:, lanes((r * 2 + i) * GROUP * HD, GROUP * HD)]
        if b == 0:
            copy = pltpu.make_async_copy(o_s.at[u, mine], there, o_l.at[i])
            copy.start()
            out_copies.append(copy)
            send(o_s.at[u, theirs], there, o_t.at[u, 0], o_r.at[2, i], sibling)
        else:
            for cc in range(2):
                send(o_s.at[u, pl.ds(cc * HALF, HALF)], there, o_t.at[u, cc], o_r.at[c, i], across[cc])

    share(0)
    share(1)
    share(2)
    share(3)
    share_queries()
    send_own(0)
    y_send(0, 0)
    send_own(1)
    y_send(1, 0)
    read_ancestors()
    build_bias()
    z_near(0)
    send_own(2)
    y_send(2, 0)
    z_near(1)
    z_far(0)
    send_own(3)
    y_send(3, 0)
    z_near(2)
    z_far(1)
    z_near(3)
    q_local.wait()
    arrived(q_s.at[0, theirs], q_r.at[2])
    rest(0)
    attend(0)
    z_far(2)
    for cc in range(2):
        arrived(q_s.at[1, pl.ds(cc * HALF, HALF)], q_r.at[cc])
    rest(1)
    attend(1)
    z_far(3)
    rest(2)
    attend(2)
    drain()
    rest(3)
    attend(3)
    drain()
    for copy in out_copies:
        copy.wait()
    for i in range(2):
        for n in range(3):
            arrived(out_ref.at[:, pl.ds(0, GROUP * HD)], o_r.at[n, i])


def local(queries, keys, values, ancestors):
    kv = pltpu.VMEM((16, 2, NODE, HD), jnp.bfloat16)
    dma = pltpu.SemaphoreType.DMA
    anywhere = pl.BlockSpec(memory_space=pl.ANY)
    return pl.pallas_call(
        kernel,
        out_shape=jax.ShapeDtypeStruct((HALF, 8192), jnp.bfloat16),
        in_specs=[anywhere] * 4,
        out_specs=anywhere,
        scratch_shapes=[
            pltpu.SMEM((4, ANC), jnp.int32), dma(()),
            kv, kv, kv, kv,
            pltpu.VMEM((2, NODE, 2048), jnp.bfloat16),
            pltpu.VMEM((4, NODE, 1024), jnp.bfloat16),
            pltpu.VMEM((2, NODE, KEYS), jnp.float32),
            dma((2, 2)), dma((4, 2, 2)), dma((4, 2, 2)), dma((1,)), dma((3,)), dma((3,)),
            dma((4, 2)), dma((4, 2)), dma((4, 2)), dma((4, 2)),
            dma((4, 4, 3)), dma((4, 16)),
            dma((2,)), dma((4, 2)), dma((3, 2)),
        ],
        compiler_params=pltpu.CompilerParams(
            collective_id=0, has_side_effects=True, vmem_limit_bytes=62 << 20),
        cost_estimate=pl.CostEstimate(
            flops=2 * 2 * 96 * 32 * 672 * 128, bytes_accessed=4 << 20, transcendentals=96 * 32 * 672),
        name="tree_attention",
    )(queries, keys, values, ancestors)


def solution(mesh):
    split = P(("dp", "tensor"), None)
    return jax.shard_map(
        local, mesh=mesh, in_specs=(split, split, split, P("dp", None)), out_specs=split, check_vma=False)
```

```python
import math

import jax
import jax.numpy as jnp
from jax import lax
from jax.experimental import pallas as pl
from jax.experimental.pallas import tpu as pltpu
from jax.sharding import PartitionSpec as P

HD = 128
NODE = 96
HALF = 48
ANC = 6
KEYS = (ANC + 1) * NODE
GROUP = 8
JOINT = 4
MESH = pl.DeviceIdType.MESH
EXP_SCALE = math.log2(math.e) / math.sqrt(HD)
UNITS = ((0, 0), (1, 0), (1, 1), (0, 1))


def kernel(q_ref, k_ref, v_ref, anc_hbm, out_ref, anc_ref, anc_sem, kv0, kv1, kv2, kv3, q_s, o_s, bias_s,
           kv_l, kv_s, kv_r, q_l, q_t, q_r, zs, zf, zr, zo, zd_s, zd_r, ys, yr, o_l, o_t, o_r):
    kv = (kv0, kv1, kv2, kv3)
    dp, t = lax.axis_index("dp"), lax.axis_index("tensor")
    x, c = t // 2, t % 2
    y, w, g = dp // 16, (dp % 16) // 4, dp % 4
    px = x + 1 - 2 * (x % 2)
    r = t % 4

    fam = [x % 2, px % 2]
    rows = [y + f * (3 - 2 * y) for f in fam]
    cols = [w + f * (3 - 2 * w) for f in fam]
    me = [rows[b] * 4 + cols[b] for b in range(2)]

    def dev(b, row, col):
        yy = row + fam[b] * (3 - 2 * row)
        ww = col + fam[b] * (3 - 2 * col)
        return (yy * 16 + ww * 4 + g, t)

    def col_at(b, i):
        return lax.rem(cols[b] + i, 4)

    sibling = (dp, x * 2 + 1 - c)
    across = [(dp, px * 2 + cc) for cc in range(2)]
    mine = pl.ds(pl.multiple_of(c * HALF, 16), HALF)
    theirs = pl.ds(pl.multiple_of((1 - c) * HALF, 16), HALF)

    def lanes(start, size):
        return pl.ds(pl.multiple_of(start, 128), size)

    def remote(src, dst, s_sem, r_sem, to):
        return pltpu.make_async_remote_copy(src, dst, s_sem, r_sem, device_id=to, device_id_type=MESH)

    sent = []

    def send(src, dst, s_sem, r_sem, to, when=None):
        copy = remote(src, dst, s_sem, r_sem, to)
        if when is None:
            copy.start()
        else:
            pl.when(when)(copy.start)
        sent.append((copy, when))

    def drain():
        for copy, when in sent:
            if when is None:
                copy.wait_send()
            else:
                pl.when(when)(copy.wait_send)
        sent.clear()

    def arrived(ref, sem, when=None):
        copy = remote(ref, ref, sem, sem, sibling)
        if when is None:
            copy.wait_recv()
        else:
            pl.when(when)(copy.wait_recv)

    anc_copy = pltpu.make_async_copy(anc_hbm, anc_ref, anc_sem)
    anc_copy.start()
    kv_local = {}
    for u in (0, 3):
        i = UNITS[u][1]
        for n, ref in enumerate((k_ref, v_ref)):
            copy = pltpu.make_async_copy(
                ref.at[:, lanes((r * 2 + i) * HD, HD)], kv[u].at[me[0], n, mine], kv_l.at[i, n])
            copy.start()
            kv_local[u, n] = copy
    q_local = pltpu.make_async_copy(q_ref.at[:, lanes(r * 2048, 2048)], q_s.at[0, mine], q_l.at[0])
    q_local.start()

    barrier = pltpu.get_barrier_semaphore()
    others = []
    for i in (1, 3):
        there = dev(0, rows[0], col_at(0, i))[0]
        others += [(there, t), (there, x * 2 + 1 - c)]
    others += [dev(0, lax.rem(rows[0] + d, 4), cols[0]) for d in (2, 1, 3)] + [*across, sibling]
    for partner in others:
        pl.semaphore_signal(barrier, inc=1, device_id=partner, device_id_type=MESH)
    pl.semaphore_wait(barrier, len(others))

    def share(u):
        b, i = UNITS[u]
        for n, ref in enumerate((k_ref, v_ref)):
            if b == 0:
                rr = x % 2 * 2 + 1 - c
                send(ref.at[:, lanes((rr * 2 + i) * HD, HD)], kv[u].at[me[0], n, mine],
                     kv_s.at[u, n, 0], kv_r.at[u, n, 0], sibling)
            else:
                for cc in range(2):
                    rr = px % 2 * 2 + cc
                    send(ref.at[:, lanes((rr * 2 + i) * HD, HD)], kv[u].at[me[0], n, mine],
                         kv_s.at[u, n, cc], kv_r.at[u, n, c], across[cc])

    def share_queries():
        for cc in range(2):
            rr = px % 2 * 2 + cc
            send(q_ref.at[:, lanes(rr * 2048, 2048)], q_s.at[1, mine], q_t.at[cc], q_r.at[c], across[cc])
        rr = x % 2 * 2 + 1 - c
        send(q_ref.at[:, lanes(rr * 2048, 2048)], q_s.at[0, mine], q_t.at[2], q_r.at[2], sibling)

    def send_raw():
        for n, to in ((0, 1), (1, 3)):
            there = dev(0, rows[0], col_at(0, to))[0]
            for cc in range(2):
                rr = x % 2 * 2 + cc
                for m, ref in enumerate((k_ref, v_ref)):
                    send(ref.at[:, lanes(rr * 2 * HD, HD)], kv[0].at[me[0], m, mine],
                         zd_s.at[n, cc, m], zd_r.at[n, m, c], (there, x * 2 + cc))

    def own_ready(u):
        b, i = UNITS[u]
        for n in range(2):
            if b == 0:
                kv_local[u, n].wait()
                arrived(kv[u].at[me[0], n, theirs], kv_r.at[u, n, 0])
            else:
                for cc in range(2):
                    arrived(kv[u].at[me[1], n, pl.ds(cc * HALF, HALF)], kv_r.at[u, n, cc])

    def y_send(u, i):
        b = UNITS[u][0]
        block = kv[u].at[rows[b] * 4 + col_at(b, i)]
        for d in (1, 2, 3):
            send(block, block, ys.at[u, i, d - 1], yr.at[u, rows[b] * 4 + col_at(b, i)],
                 dev(b, lax.rem(rows[b] + d, 4), cols[b]), rows[b] + d < 4)

    def send_own(u, when=None):
        b = UNITS[u][0]
        block = kv[u].at[me[b]]
        send(block, block, zs.at[u, 0], zr.at[u, 0], dev(b, rows[b], col_at(b, 1)), when)
        send(block, block, zs.at[u, 1], zr.at[u, 1], dev(b, rows[b], col_at(b, 3)), when)

    def z_near(u):
        b = UNITS[u][0]
        for n, i in ((0, 3), (1, 1)):
            block = kv[u].at[rows[b] * 4 + col_at(b, i)]
            if u == 0:
                for m in range(2):
                    for cc in range(2):
                        arrived(block.at[m, pl.ds(cc * HALF, HALF)], zd_r.at[n, m, cc])
            else:
                arrived(block, zr.at[u, n])
            y_send(u, i)

    def z_pass(u):
        b = UNITS[u][0]
        for n, i, to in ((0, 3, 1), (1, 1, 3)):
            block = kv[u].at[rows[b] * 4 + col_at(b, i), n]
            send(block, block, zf.at[u, n], zo.at[u, n], dev(b, rows[b], col_at(b, to)))

    def z_far(u):
        b = UNITS[u][0]
        block = kv[u].at[rows[b] * 4 + col_at(b, 2)]
        for n in range(2):
            arrived(block.at[n], zo.at[u, n])
        y_send(u, 2)

    def rest(u):
        b = UNITS[u][0]
        for row in range(3):
            for i in (0, 3, 1, 2):
                slot = row * 4 + col_at(b, i)
                arrived(kv[u].at[slot], yr.at[u, slot], rows[b] > row)

    places, listed = [], []

    def read_ancestors():
        anc_copy.wait()
        listed.extend([[anc_ref[x if b == 0 else px, i] for i in range(ANC)] for b in range(2)])
        for b in range(2):
            found = []
            for a in listed[b]:
                a0 = jnp.maximum(a, 0)
                ay, aw = a0 >> 6, (a0 >> 4) & 3
                ay = ay + fam[b] * (3 - 2 * ay)
                aw = aw + fam[b] * (3 - 2 * aw)
                found.append(jnp.where(a >= 0, ay * 4 + aw, me[b]))
            places.append(found + [me[b]])

    def build_bias():
        at_row = lax.broadcasted_iota(jnp.int32, (NODE, KEYS), 0)
        at = lax.broadcasted_iota(jnp.int32, (NODE, KEYS), 1)
        causal = jnp.where(at - ANC * NODE > at_row, -1e30, 0.0)
        for b in range(2):
            bias = causal
            for i, a in enumerate(listed[b]):
                inside = (at >= NODE * i) & (at < NODE * (i + 1))
                bias = jnp.where(inside, jnp.where(a >= 0, 0.0, -1e30), bias)
            bias_s[b] = bias

    def outputs(u):
        b, i = UNITS[u]
        there = out_ref.at[:, lanes((r * 2 + i) * GROUP * HD, GROUP * HD)]
        if b == 0:
            return (remote(o_s.at[u, theirs], there, o_t.at[u, 0], o_r.at[2, i], sibling),
                    pltpu.make_async_copy(o_s.at[u, mine], there, o_l.at[i]))
        return [remote(o_s.at[u, pl.ds(cc * HALF, HALF)], there, o_t.at[u, cc], o_r.at[c, i], across[cc])
                for cc in range(2)]

    def attend(u):
        b, i = UNITS[u]
        keys = jnp.concatenate([kv[u][s, 0] for s in places[b]], axis=0)
        values = jnp.concatenate([kv[u][s, 1] for s in places[b]], axis=0)
        for first in range(0, GROUP, JOINT):
            at = [(i * GROUP + first + j) * HD for j in range(JOINT)]
            queries = jnp.concatenate([q_s[b, :, a:a + HD] for a in at], axis=0)
            scores = lax.dot_general(queries, keys, (((1,), (1,)), ((), ())), preferred_element_type=jnp.float32)
            scores = (scores.reshape(JOINT, NODE, KEYS) + bias_s[b][None]).reshape(JOINT * NODE, KEYS)
            top = jnp.max(scores, axis=-1, keepdims=True)
            weights = jnp.exp2((scores - top) * EXP_SCALE)
            total = jnp.sum(weights, axis=-1, keepdims=True)
            mixed = jnp.dot(weights.astype(jnp.bfloat16), values, preferred_element_type=jnp.float32)
            mixed = (mixed / total).astype(jnp.bfloat16)
            for j in range(JOINT):
                o_s[u, :, (first + j) * HD:(first + j + 1) * HD] = mixed[j * NODE:(j + 1) * NODE]
        for copy in outputs(u):
            copy.start()

    first = g == 0
    send_raw()
    share(0)
    share(1)
    share(2)
    share(3)
    share_queries()
    own_ready(0)
    y_send(0, 0)
    own_ready(1)
    send_own(1)
    y_send(1, 0)
    own_ready(2)
    send_own(2, first)
    own_ready(3)
    send_own(3, first)
    read_ancestors()
    build_bias()
    z_near(0)
    send_own(2, jnp.logical_not(first))
    y_send(2, 0)
    z_near(1)
    z_pass(1)
    send_own(3, jnp.logical_not(first))
    y_send(3, 0)
    z_near(2)
    z_pass(2)
    z_far(1)
    z_pass(0)
    z_near(3)
    z_pass(3)
    z_far(2)
    for cc in range(2):
        arrived(q_s.at[1, pl.ds(cc * HALF, HALF)], q_r.at[cc])
    rest(1)
    attend(1)
    z_far(0)
    q_local.wait()
    arrived(q_s.at[0, theirs], q_r.at[2])
    pl.when(rows[0] == 0)(lambda: attend(0))
    rest(2)
    attend(2)
    z_far(3)
    rest(0)
    pl.when(rows[0] > 0)(lambda: attend(0))
    drain()
    rest(3)
    attend(3)
    drain()
    for u in range(4):
        first_copy, second_copy = outputs(u)
        first_copy.wait_send()
        if UNITS[u][0] == 0:
            second_copy.wait()
        else:
            second_copy.wait_send()
    for i in range(2):
        for n in range(3):
            arrived(out_ref.at[:, pl.ds(0, GROUP * HD)], o_r.at[n, i])


def local(queries, keys, values, ancestors):
    kv = pltpu.VMEM((16, 2, NODE, HD), jnp.bfloat16)
    dma = pltpu.SemaphoreType.DMA
    anywhere = pl.BlockSpec(memory_space=pl.ANY)
    return pl.pallas_call(
        kernel,
        out_shape=jax.ShapeDtypeStruct((HALF, 8192), jnp.bfloat16),
        in_specs=[anywhere] * 4,
        out_specs=anywhere,
        scratch_shapes=[
            pltpu.SMEM((4, ANC), jnp.int32), dma(()),
            kv, kv, kv, kv,
            pltpu.VMEM((2, NODE, 2048), jnp.bfloat16),
            pltpu.VMEM((4, NODE, 1024), jnp.bfloat16),
            pltpu.VMEM((2, NODE, KEYS), jnp.float32),
            dma((2, 2)), dma((4, 2, 2)), dma((4, 2, 2)), dma((1,)), dma((3,)), dma((3,)),
            dma((4, 2)), dma((4, 2)), dma((4, 2)), dma((4, 2)), dma((2, 2, 2)), dma((2, 2, 2)),
            dma((4, 4, 3)), dma((4, 16)),
            dma((2,)), dma((4, 2)), dma((3, 2)),
        ],
        compiler_params=pltpu.CompilerParams(
            collective_id=0, has_side_effects=True, vmem_limit_bytes=62 << 20),
        cost_estimate=pl.CostEstimate(
            flops=2 * 2 * 96 * 32 * 672 * 128, bytes_accessed=4 << 20, transcendentals=96 * 32 * 672),
        name="tree_attention",
    )(queries, keys, values, ancestors)


def solution(mesh):
    split = P(("dp", "tensor"), None)
    return jax.shard_map(
        local, mesh=mesh, in_specs=(split, split, split, P("dp", None)), out_specs=split, check_vma=False)
```

```python
import math

import jax
import jax.numpy as jnp
from jax import lax
from jax.experimental import pallas as pl
from jax.experimental.pallas import tpu as pltpu
from jax.sharding import PartitionSpec as P

HD = 128
NODE = 96
HALF = 48
ANC = 6
KEYS = (ANC + 1) * NODE
GROUP = 8
JOINT = 4
MESH = pl.DeviceIdType.MESH
EXP_SCALE = math.log2(math.e) / math.sqrt(HD)
UNITS = ((0, 0), (1, 0), (1, 1), (0, 1))


def kernel(q_ref, k_ref, v_ref, anc_hbm, out_ref, anc_ref, anc_sem, kv0, kv1, kv2, kv3, q_s, o_s, bias_s,
           kv_l, kv_s, kv_r, q_l, q_t, q_r, zs, zf, zr, zo, zd_s, zd_r, ys, yr, o_l, o_t, o_r):
    kv = (kv0, kv1, kv2, kv3)
    dp, t = lax.axis_index("dp"), lax.axis_index("tensor")
    x, c = t // 2, t % 2
    y, w, g = dp // 16, (dp % 16) // 4, dp % 4
    px = x + 1 - 2 * (x % 2)
    r = t % 4

    fam = [x % 2, px % 2]
    rows = [y + f * (3 - 2 * y) for f in fam]
    cols = [w + f * (3 - 2 * w) for f in fam]
    me = [rows[b] * 4 + cols[b] for b in range(2)]

    def dev(b, row, col):
        yy = row + fam[b] * (3 - 2 * row)
        ww = col + fam[b] * (3 - 2 * col)
        return (yy * 16 + ww * 4 + g, t)

    def col_at(b, i):
        return lax.rem(cols[b] + i, 4)

    sibling = (dp, x * 2 + 1 - c)
    across = [(dp, px * 2 + cc) for cc in range(2)]
    mine = pl.ds(pl.multiple_of(c * HALF, 16), HALF)
    theirs = pl.ds(pl.multiple_of((1 - c) * HALF, 16), HALF)

    def lanes(start, size):
        return pl.ds(pl.multiple_of(start, 128), size)

    def remote(src, dst, s_sem, r_sem, to):
        return pltpu.make_async_remote_copy(src, dst, s_sem, r_sem, device_id=to, device_id_type=MESH)

    sent = []

    def send(src, dst, s_sem, r_sem, to, when=None):
        copy = remote(src, dst, s_sem, r_sem, to)
        if when is None:
            copy.start()
        else:
            pl.when(when)(copy.start)
        sent.append((copy, when))

    def drain():
        for copy, when in sent:
            if when is None:
                copy.wait_send()
            else:
                pl.when(when)(copy.wait_send)
        sent.clear()

    def arrived(ref, sem, when=None):
        copy = remote(ref, ref, sem, sem, sibling)
        if when is None:
            copy.wait_recv()
        else:
            pl.when(when)(copy.wait_recv)

    anc_copy = pltpu.make_async_copy(anc_hbm, anc_ref, anc_sem)
    anc_copy.start()
    kv_local = {}
    for u in (0, 3):
        i = UNITS[u][1]
        for n, ref in enumerate((k_ref, v_ref)):
            copy = pltpu.make_async_copy(
                ref.at[:, lanes((r * 2 + i) * HD, HD)], kv[u].at[me[0], n, mine], kv_l.at[i, n])
            copy.start()
            kv_local[u, n] = copy
    q_local = pltpu.make_async_copy(q_ref.at[:, lanes(r * 2048, 2048)], q_s.at[0, mine], q_l.at[0])
    q_local.start()

    barrier = pltpu.get_barrier_semaphore()
    others = []
    for i in (1, 3):
        there = dev(0, rows[0], col_at(0, i))[0]
        others += [(there, t), (there, x * 2 + 1 - c)]
    others += [dev(0, lax.rem(rows[0] + d, 4), cols[0]) for d in (2, 1, 3)] + [*across, sibling]
    for partner in others:
        pl.semaphore_signal(barrier, inc=1, device_id=partner, device_id_type=MESH)
    pl.semaphore_wait(barrier, len(others))

    def share(u):
        b, i = UNITS[u]
        for n, ref in enumerate((k_ref, v_ref)):
            if b == 0:
                rr = x % 2 * 2 + 1 - c
                send(ref.at[:, lanes((rr * 2 + i) * HD, HD)], kv[u].at[me[0], n, mine],
                     kv_s.at[u, n, 0], kv_r.at[u, n, 0], sibling)
            else:
                for cc in range(2):
                    rr = px % 2 * 2 + cc
                    send(ref.at[:, lanes((rr * 2 + i) * HD, HD)], kv[u].at[me[0], n, mine],
                         kv_s.at[u, n, cc], kv_r.at[u, n, c], across[cc])

    def share_queries():
        for cc in range(2):
            rr = px % 2 * 2 + cc
            send(q_ref.at[:, lanes(rr * 2048, 2048)], q_s.at[1, mine], q_t.at[cc], q_r.at[c], across[cc])
        rr = x % 2 * 2 + 1 - c
        send(q_ref.at[:, lanes(rr * 2048, 2048)], q_s.at[0, mine], q_t.at[2], q_r.at[2], sibling)

    def send_raw():
        for n, to in ((0, 1), (1, 3)):
            there = dev(0, rows[0], col_at(0, to))[0]
            for cc in range(2):
                rr = x % 2 * 2 + cc
                for m, ref in enumerate((k_ref, v_ref)):
                    send(ref.at[:, lanes(rr * 2 * HD, HD)], kv[0].at[me[0], m, mine],
                         zd_s.at[n, cc, m], zd_r.at[n, m, c], (there, x * 2 + cc))

    def own_ready(u):
        b, i = UNITS[u]
        for n in range(2):
            if b == 0:
                kv_local[u, n].wait()
                arrived(kv[u].at[me[0], n, theirs], kv_r.at[u, n, 0])
            else:
                for cc in range(2):
                    arrived(kv[u].at[me[1], n, pl.ds(cc * HALF, HALF)], kv_r.at[u, n, cc])

    def y_send(u, i):
        b = UNITS[u][0]
        block = kv[u].at[rows[b] * 4 + col_at(b, i)]
        for d in (1, 2, 3):
            send(block, block, ys.at[u, i, d - 1], yr.at[u, rows[b] * 4 + col_at(b, i)],
                 dev(b, lax.rem(rows[b] + d, 4), cols[b]), rows[b] + d < 4)

    def send_own(u, when=None):
        b = UNITS[u][0]
        block = kv[u].at[me[b]]
        send(block, block, zs.at[u, 0], zr.at[u, 0], dev(b, rows[b], col_at(b, 1)), when)
        send(block, block, zs.at[u, 1], zr.at[u, 1], dev(b, rows[b], col_at(b, 3)), when)

    def z_near(u):
        b = UNITS[u][0]
        for n, i in ((0, 3), (1, 1)):
            block = kv[u].at[rows[b] * 4 + col_at(b, i)]
            if u == 0:
                for m in range(2):
                    for cc in range(2):
                        arrived(block.at[m, pl.ds(cc * HALF, HALF)], zd_r.at[n, m, cc])
            else:
                arrived(block, zr.at[u, n])
            y_send(u, i)

    def z_pass(u):
        b = UNITS[u][0]
        for n, i, to in ((0, 3, 1), (1, 1, 3)):
            block = kv[u].at[rows[b] * 4 + col_at(b, i), n]
            send(block, block, zf.at[u, n], zo.at[u, n], dev(b, rows[b], col_at(b, to)))

    def z_far(u):
        b = UNITS[u][0]
        block = kv[u].at[rows[b] * 4 + col_at(b, 2)]
        for n in range(2):
            arrived(block.at[n], zo.at[u, n])
        y_send(u, 2)

    def rest(u):
        b = UNITS[u][0]
        for row in range(3):
            for i in (0, 3, 1, 2):
                slot = row * 4 + col_at(b, i)
                arrived(kv[u].at[slot], yr.at[u, slot], rows[b] > row)

    places, listed = [], []

    def read_ancestors():
        anc_copy.wait()
        listed.extend([[anc_ref[x if b == 0 else px, i] for i in range(ANC)] for b in range(2)])
        for b in range(2):
            found = []
            for a in listed[b]:
                a0 = jnp.maximum(a, 0)
                ay, aw = a0 >> 6, (a0 >> 4) & 3
                ay = ay + fam[b] * (3 - 2 * ay)
                aw = aw + fam[b] * (3 - 2 * aw)
                found.append(jnp.where(a >= 0, ay * 4 + aw, me[b]))
            places.append(found + [me[b]])

    def build_bias():
        at_row = lax.broadcasted_iota(jnp.int32, (NODE, KEYS), 0)
        at = lax.broadcasted_iota(jnp.int32, (NODE, KEYS), 1)
        causal = jnp.where(at - ANC * NODE > at_row, -1e30, 0.0)
        for b in range(2):
            bias = causal
            for i, a in enumerate(listed[b]):
                inside = (at >= NODE * i) & (at < NODE * (i + 1))
                bias = jnp.where(inside, jnp.where(a >= 0, 0.0, -1e30), bias)
            bias_s[b] = bias

    def outputs(u):
        b, i = UNITS[u]
        there = out_ref.at[:, lanes((r * 2 + i) * GROUP * HD, GROUP * HD)]
        if b == 0:
            return (remote(o_s.at[u, theirs], there, o_t.at[u, 0], o_r.at[2, i], sibling),
                    pltpu.make_async_copy(o_s.at[u, mine], there, o_l.at[i]))
        return [remote(o_s.at[u, pl.ds(cc * HALF, HALF)], there, o_t.at[u, cc], o_r.at[c, i], across[cc])
                for cc in range(2)]

    def attend(u):
        b, i = UNITS[u]
        keys = jnp.concatenate([kv[u][s, 0] for s in places[b]], axis=0)
        values = jnp.concatenate([kv[u][s, 1] for s in places[b]], axis=0)
        for first in range(0, GROUP, JOINT):
            at = [(i * GROUP + first + j) * HD for j in range(JOINT)]
            queries = jnp.concatenate([q_s[b, :, a:a + HD] for a in at], axis=0)
            scores = lax.dot_general(queries, keys, (((1,), (1,)), ((), ())), preferred_element_type=jnp.float32)
            scores = (scores.reshape(JOINT, NODE, KEYS) + bias_s[b][None]).reshape(JOINT * NODE, KEYS)
            top = jnp.max(scores, axis=-1, keepdims=True)
            weights = jnp.exp2((scores - top) * EXP_SCALE)
            total = jnp.sum(weights, axis=-1, keepdims=True)
            mixed = jnp.dot(weights.astype(jnp.bfloat16), values, preferred_element_type=jnp.float32)
            mixed = (mixed / total).astype(jnp.bfloat16)
            for j in range(JOINT):
                o_s[u, :, (first + j) * HD:(first + j + 1) * HD] = mixed[j * NODE:(j + 1) * NODE]
        for copy in outputs(u):
            copy.start()

    first = g == 0
    send_raw()
    share(0)
    share(1)
    share(2)
    share(3)
    share_queries()
    own_ready(0)
    y_send(0, 0)
    own_ready(1)
    send_own(1)
    y_send(1, 0)
    own_ready(2)
    send_own(2, first)
    own_ready(3)
    send_own(3, first)
    read_ancestors()
    build_bias()
    z_near(0)
    send_own(2, jnp.logical_not(first))
    y_send(2, 0)
    z_near(1)
    z_pass(1)
    send_own(3, jnp.logical_not(first))
    y_send(3, 0)
    z_near(2)
    z_pass(2)
    z_far(1)
    z_pass(0)
    z_near(3)
    z_pass(3)
    z_far(2)
    for cc in range(2):
        arrived(q_s.at[1, pl.ds(cc * HALF, HALF)], q_r.at[cc])
    rest(1)
    attend(1)
    z_far(0)
    q_local.wait()
    arrived(q_s.at[0, theirs], q_r.at[2])
    pl.when(rows[0] == 0)(lambda: attend(0))
    rest(2)
    attend(2)
    z_far(3)
    rest(0)
    pl.when(rows[0] > 0)(lambda: attend(0))
    drain()
    rest(3)
    attend(3)
    drain()
    for u in range(4):
        first_copy, second_copy = outputs(u)
        first_copy.wait_send()
        if UNITS[u][0] == 0:
            second_copy.wait()
        else:
            second_copy.wait_send()
    for i in range(2):
        for n in range(3):
            arrived(out_ref.at[:, pl.ds(0, GROUP * HD)], o_r.at[n, i])


def local(queries, keys, values, ancestors):
    kv = pltpu.VMEM((16, 2, NODE, HD), jnp.bfloat16)
    dma = pltpu.SemaphoreType.DMA
    anywhere = pl.BlockSpec(memory_space=pl.ANY)
    return pl.pallas_call(
        kernel,
        out_shape=pltpu.VMEM((HALF, 8192), jnp.bfloat16),
        in_specs=[anywhere] * 4,
        out_specs=anywhere,
        scratch_shapes=[
            pltpu.SMEM((4, ANC), jnp.int32), dma(()),
            kv, kv, kv, kv,
            pltpu.VMEM((2, NODE, 2048), jnp.bfloat16),
            pltpu.VMEM((4, NODE, 1024), jnp.bfloat16),
            pltpu.VMEM((2, NODE, KEYS), jnp.float32),
            dma((2, 2)), dma((4, 2, 2)), dma((4, 2, 2)), dma((1,)), dma((3,)), dma((3,)),
            dma((4, 2)), dma((4, 2)), dma((4, 2)), dma((4, 2)), dma((2, 2, 2)), dma((2, 2, 2)),
            dma((4, 4, 3)), dma((4, 16)),
            dma((2,)), dma((4, 2)), dma((3, 2)),
        ],
        compiler_params=pltpu.CompilerParams(
            collective_id=0, has_side_effects=True, vmem_limit_bytes=62 << 20),
        cost_estimate=pl.CostEstimate(
            flops=2 * 2 * 96 * 32 * 672 * 128, bytes_accessed=4 << 20, transcendentals=96 * 32 * 672),
        name="tree_attention",
    )(queries, keys, values, ancestors)


def solution(mesh):
    split = P(("dp", "tensor"), None)
    return jax.shard_map(
        local, mesh=mesh, in_specs=(split, split, split, P("dp", None)), out_specs=split, check_vma=False)
```

```python
import math

import jax
import jax.numpy as jnp
from jax import lax
from jax.experimental import pallas as pl
from jax.experimental.pallas import tpu as pltpu
from jax.sharding import PartitionSpec as P

HD = 128
NODE = 96
HALF = 48
ANC = 6
KEYS = (ANC + 1) * NODE
GROUP = 8
JOINT = 4
MESH = pl.DeviceIdType.MESH
EXP_SCALE = math.log2(math.e) / math.sqrt(HD)
UNITS = ((0, 0), (1, 0), (1, 1), (0, 1))


def kernel(q_ref, k_ref, v_ref, anc_hbm, out_ref, anc_ref, anc_sem, kv0, kv1, kv2, kv3, q_s, o_s, bias_s,
           kv_l, kv_s, kv_r, q_l, q_t, q_r, zs, zf, zr, zo, zd_s, zd_r, ys, yr, o_l, o_t, o_r):
    kv = (kv0, kv1, kv2, kv3)
    dp, t = lax.axis_index("dp"), lax.axis_index("tensor")
    x, c = t // 2, t % 2
    y, w, g = dp // 16, (dp % 16) // 4, dp % 4
    px = x + 1 - 2 * (x % 2)
    r = t % 4

    fam = [x % 2, px % 2]
    rows = [y + f * (3 - 2 * y) for f in fam]
    cols = [w + f * (3 - 2 * w) for f in fam]
    me = [rows[b] * 4 + cols[b] for b in range(2)]

    def dev(b, row, col):
        yy = row + fam[b] * (3 - 2 * row)
        ww = col + fam[b] * (3 - 2 * col)
        return (yy * 16 + ww * 4 + g, t)

    def col_at(b, i):
        return lax.rem(cols[b] + i, 4)

    sibling = (dp, x * 2 + 1 - c)
    across = [(dp, px * 2 + cc) for cc in range(2)]
    mine = pl.ds(pl.multiple_of(c * HALF, 16), HALF)
    theirs = pl.ds(pl.multiple_of((1 - c) * HALF, 16), HALF)

    def lanes(start, size):
        return pl.ds(pl.multiple_of(start, 128), size)

    def remote(src, dst, s_sem, r_sem, to):
        return pltpu.make_async_remote_copy(src, dst, s_sem, r_sem, device_id=to, device_id_type=MESH)

    sent = []

    def send(src, dst, s_sem, r_sem, to, when=None):
        copy = remote(src, dst, s_sem, r_sem, to)
        if when is None:
            copy.start()
        else:
            pl.when(when)(copy.start)
        sent.append((copy, when))

    def drain():
        for copy, when in sent:
            if when is None:
                copy.wait_send()
            else:
                pl.when(when)(copy.wait_send)
        sent.clear()

    def arrived(ref, sem, when=None):
        copy = remote(ref, ref, sem, sem, sibling)
        if when is None:
            copy.wait_recv()
        else:
            pl.when(when)(copy.wait_recv)

    anc_copy = pltpu.make_async_copy(anc_hbm, anc_ref, anc_sem)
    anc_copy.start()
    kv_local = {}
    for u in (0, 3):
        i = UNITS[u][1]
        for n, ref in enumerate((k_ref, v_ref)):
            copy = pltpu.make_async_copy(
                ref.at[:, lanes((r * 2 + i) * HD, HD)], kv[u].at[me[0], n, mine], kv_l.at[i, n])
            copy.start()
            kv_local[u, n] = copy
    q_local = pltpu.make_async_copy(q_ref.at[:, lanes(r * 2048, 2048)], q_s.at[0, mine], q_l.at[0])
    q_local.start()

    barrier = pltpu.get_barrier_semaphore()
    others = []
    for i in (1, 3):
        there = dev(0, rows[0], col_at(0, i))[0]
        others += [(there, t), (there, x * 2 + 1 - c)]
    others += [dev(0, lax.rem(rows[0] + d, 4), cols[0]) for d in (2, 1, 3)] + [*across, sibling]
    for partner in others:
        pl.semaphore_signal(barrier, inc=1, device_id=partner, device_id_type=MESH)
    pl.semaphore_wait(barrier, len(others))

    def share(u):
        b, i = UNITS[u]
        for n, ref in enumerate((k_ref, v_ref)):
            if b == 0:
                rr = x % 2 * 2 + 1 - c
                send(ref.at[:, lanes((rr * 2 + i) * HD, HD)], kv[u].at[me[0], n, mine],
                     kv_s.at[u, n, 0], kv_r.at[u, n, 0], sibling)
            else:
                for cc in range(2):
                    rr = px % 2 * 2 + cc
                    send(ref.at[:, lanes((rr * 2 + i) * HD, HD)], kv[u].at[me[0], n, mine],
                         kv_s.at[u, n, cc], kv_r.at[u, n, c], across[cc])

    def share_queries():
        for cc in range(2):
            rr = px % 2 * 2 + cc
            send(q_ref.at[:, lanes(rr * 2048, 2048)], q_s.at[1, mine], q_t.at[cc], q_r.at[c], across[cc])
        rr = x % 2 * 2 + 1 - c
        send(q_ref.at[:, lanes(rr * 2048, 2048)], q_s.at[0, mine], q_t.at[2], q_r.at[2], sibling)

    def send_raw():
        for n, to in ((0, 1), (1, 3)):
            there = dev(0, rows[0], col_at(0, to))[0]
            for cc in range(2):
                rr = x % 2 * 2 + cc
                for m, ref in enumerate((k_ref, v_ref)):
                    send(ref.at[:, lanes(rr * 2 * HD, HD)], kv[0].at[me[0], m, mine],
                         zd_s.at[n, cc, m], zd_r.at[n, m, c], (there, x * 2 + cc))

    def own_ready(u):
        b, i = UNITS[u]
        for n in range(2):
            if b == 0:
                kv_local[u, n].wait()
                arrived(kv[u].at[me[0], n, theirs], kv_r.at[u, n, 0])
            else:
                for cc in range(2):
                    arrived(kv[u].at[me[1], n, pl.ds(cc * HALF, HALF)], kv_r.at[u, n, cc])

    def y_send(u, i):
        b = UNITS[u][0]
        block = kv[u].at[rows[b] * 4 + col_at(b, i)]
        for d in (1, 2, 3):
            send(block, block, ys.at[u, i, d - 1], yr.at[u, rows[b] * 4 + col_at(b, i)],
                 dev(b, lax.rem(rows[b] + d, 4), cols[b]), rows[b] + d < 4)

    def send_own(u, when=None):
        b = UNITS[u][0]
        block = kv[u].at[me[b]]
        send(block, block, zs.at[u, 0], zr.at[u, 0], dev(b, rows[b], col_at(b, 1)), when)
        send(block, block, zs.at[u, 1], zr.at[u, 1], dev(b, rows[b], col_at(b, 3)), when)

    def z_near(u):
        b = UNITS[u][0]
        for n, i, to in ((0, 3, 1), (1, 1, 3)):
            block = kv[u].at[rows[b] * 4 + col_at(b, i)]
            if u == 0:
                for m in range(2):
                    for cc in range(2):
                        arrived(block.at[m, pl.ds(cc * HALF, HALF)], zd_r.at[n, m, cc])
            else:
                arrived(block, zr.at[u, n])
            y_send(u, i)
            if u:
                pass_half(u, n, i, to)

    def pass_half(u, n, i, to):
        b = UNITS[u][0]
        block = kv[u].at[rows[b] * 4 + col_at(b, i), n]
        send(block, block, zf.at[u, n], zo.at[u, n], dev(b, rows[b], col_at(b, to)))

    def z_pass(u):
        for n, i, to in ((0, 3, 1), (1, 1, 3)):
            pass_half(u, n, i, to)

    def z_far(u):
        b = UNITS[u][0]
        block = kv[u].at[rows[b] * 4 + col_at(b, 2)]
        for n in range(2):
            arrived(block.at[n], zo.at[u, n])
        y_send(u, 2)

    def rest(u):
        b = UNITS[u][0]
        for row in range(3):
            for i in (0, 3, 1, 2):
                slot = row * 4 + col_at(b, i)
                arrived(kv[u].at[slot], yr.at[u, slot], rows[b] > row)

    places, listed = [], []

    def read_ancestors():
        anc_copy.wait()
        listed.extend([[anc_ref[x if b == 0 else px, i] for i in range(ANC)] for b in range(2)])
        for b in range(2):
            found = []
            for a in listed[b]:
                a0 = jnp.maximum(a, 0)
                ay, aw = a0 >> 6, (a0 >> 4) & 3
                ay = ay + fam[b] * (3 - 2 * ay)
                aw = aw + fam[b] * (3 - 2 * aw)
                found.append(jnp.where(a >= 0, ay * 4 + aw, me[b]))
            places.append(found + [me[b]])

    def build_bias():
        at_row = lax.broadcasted_iota(jnp.int32, (NODE, KEYS), 0)
        at = lax.broadcasted_iota(jnp.int32, (NODE, KEYS), 1)
        causal = jnp.where(at - ANC * NODE > at_row, -1e30, 0.0)
        for b in range(2):
            bias = causal
            for i, a in enumerate(listed[b]):
                inside = (at >= NODE * i) & (at < NODE * (i + 1))
                bias = jnp.where(inside, jnp.where(a >= 0, 0.0, -1e30), bias)
            bias_s[b] = bias

    def outputs(u):
        b, i = UNITS[u]
        there = out_ref.at[:, lanes((r * 2 + i) * GROUP * HD, GROUP * HD)]
        if b == 0:
            return (remote(o_s.at[u, theirs], there, o_t.at[u, 0], o_r.at[2, i], sibling),
                    pltpu.make_async_copy(o_s.at[u, mine], there, o_l.at[i]))
        return [remote(o_s.at[u, pl.ds(cc * HALF, HALF)], there, o_t.at[u, cc], o_r.at[c, i], across[cc])
                for cc in range(2)]

    def attend(u):
        b, i = UNITS[u]
        keys = jnp.concatenate([kv[u][s, 0] for s in places[b]], axis=0)
        values = jnp.concatenate([kv[u][s, 1] for s in places[b]], axis=0)
        for first in range(0, GROUP, JOINT):
            at = [(i * GROUP + first + j) * HD for j in range(JOINT)]
            queries = jnp.concatenate([q_s[b, :, a:a + HD] for a in at], axis=0)
            scores = lax.dot_general(queries, keys, (((1,), (1,)), ((), ())), preferred_element_type=jnp.float32)
            scores = (scores.reshape(JOINT, NODE, KEYS) + bias_s[b][None]).reshape(JOINT * NODE, KEYS)
            top = jnp.max(scores, axis=-1, keepdims=True)
            weights = jnp.exp2((scores - top) * EXP_SCALE)
            total = jnp.sum(weights, axis=-1, keepdims=True)
            mixed = jnp.dot(weights.astype(jnp.bfloat16), values, preferred_element_type=jnp.float32)
            mixed = (mixed / total).astype(jnp.bfloat16)
            for j in range(JOINT):
                o_s[u, :, (first + j) * HD:(first + j + 1) * HD] = mixed[j * NODE:(j + 1) * NODE]
        for copy in outputs(u):
            copy.start()

    first = (g == 0) & (w > 0)
    send_raw()
    share(0)
    share(1)
    share(2)
    share(3)
    share_queries()
    own_ready(0)
    y_send(0, 0)
    own_ready(1)
    send_own(1)
    y_send(1, 0)
    own_ready(2)
    send_own(2, first)
    own_ready(3)
    send_own(3, first)
    read_ancestors()
    build_bias()
    z_near(0)
    send_own(2, jnp.logical_not(first))
    y_send(2, 0)
    z_near(1)
    send_own(3, jnp.logical_not(first))
    y_send(3, 0)
    z_near(2)
    z_far(1)
    z_pass(0)
    z_near(3)
    z_far(2)
    for cc in range(2):
        arrived(q_s.at[1, pl.ds(cc * HALF, HALF)], q_r.at[cc])
    rest(1)
    attend(1)
    z_far(0)
    q_local.wait()
    arrived(q_s.at[0, theirs], q_r.at[2])
    pl.when(rows[0] == 0)(lambda: attend(0))
    rest(2)
    attend(2)
    z_far(3)
    rest(0)
    pl.when(rows[0] > 0)(lambda: attend(0))
    drain()
    rest(3)
    attend(3)
    drain()
    for u in range(4):
        first_copy, second_copy = outputs(u)
        first_copy.wait_send()
        if UNITS[u][0] == 0:
            second_copy.wait()
        else:
            second_copy.wait_send()
    for i in range(2):
        for n in range(3):
            arrived(out_ref.at[:, pl.ds(0, GROUP * HD)], o_r.at[n, i])


def local(queries, keys, values, ancestors):
    kv = pltpu.VMEM((16, 2, NODE, HD), jnp.bfloat16)
    dma = pltpu.SemaphoreType.DMA
    anywhere = pl.BlockSpec(memory_space=pl.ANY)
    return pl.pallas_call(
        kernel,
        out_shape=pltpu.VMEM((HALF, 8192), jnp.bfloat16),
        in_specs=[anywhere] * 4,
        out_specs=anywhere,
        scratch_shapes=[
            pltpu.SMEM((4, ANC), jnp.int32), dma(()),
            kv, kv, kv, kv,
            pltpu.VMEM((2, NODE, 2048), jnp.bfloat16),
            pltpu.VMEM((4, NODE, 1024), jnp.bfloat16),
            pltpu.VMEM((2, NODE, KEYS), jnp.float32),
            dma((2, 2)), dma((4, 2, 2)), dma((4, 2, 2)), dma((1,)), dma((3,)), dma((3,)),
            dma((4, 2)), dma((4, 2)), dma((4, 2)), dma((4, 2)), dma((2, 2, 2)), dma((2, 2, 2)),
            dma((4, 4, 3)), dma((4, 16)),
            dma((2,)), dma((4, 2)), dma((3, 2)),
        ],
        compiler_params=pltpu.CompilerParams(
            collective_id=0, has_side_effects=True, vmem_limit_bytes=62 << 20),
        cost_estimate=pl.CostEstimate(
            flops=2 * 2 * 96 * 32 * 672 * 128, bytes_accessed=4 << 20, transcendentals=96 * 32 * 672),
        name="tree_attention",
    )(queries, keys, values, ancestors)


def solution(mesh):
    split = P(("dp", "tensor"), None)
    return jax.shard_map(
        local, mesh=mesh, in_specs=(split, split, split, P("dp", None)), out_specs=split, check_vma=False)
```

```python
import math

import jax
import jax.numpy as jnp
from jax import lax
from jax.experimental import pallas as pl
from jax.experimental.pallas import tpu as pltpu
from jax.sharding import PartitionSpec as P

HD = 128
NODE = 96
HALF = 48
ANC = 6
KEYS = (ANC + 1) * NODE
GROUP = 8
JOINT = 4
MESH = pl.DeviceIdType.MESH
EXP_SCALE = math.log2(math.e) / math.sqrt(HD)
UNITS = ((0, 0), (1, 0), (1, 1), (0, 1))


def kernel(q_ref, k_ref, v_ref, anc_hbm, out_ref, anc_ref, anc_sem, kv0, kv1, kv2, kv3, q_s, o_s, bias_s,
           kv_l, kv_s, kv_r, q_l, q_t, q_r, zs, zf, zr, zo, zd_s, zd_r, ys, yr, o_l, o_t, o_r):
    kv = (kv0, kv1, kv2, kv3)
    dp, t = lax.axis_index("dp"), lax.axis_index("tensor")
    x, c = t // 2, t % 2
    y, w, g = dp // 16, (dp % 16) // 4, dp % 4
    px = x + 1 - 2 * (x % 2)
    r = t % 4

    fam = [x % 2, px % 2]
    rows = [y + f * (3 - 2 * y) for f in fam]
    cols = [w + f * (3 - 2 * w) for f in fam]
    me = [rows[b] * 4 + cols[b] for b in range(2)]

    def dev(b, row, col):
        yy = row + fam[b] * (3 - 2 * row)
        ww = col + fam[b] * (3 - 2 * col)
        return (yy * 16 + ww * 4 + g, t)

    def col_at(b, i):
        return lax.rem(cols[b] + i, 4)

    sibling = (dp, x * 2 + 1 - c)
    across = [(dp, px * 2 + cc) for cc in range(2)]
    mine = pl.ds(pl.multiple_of(c * HALF, 16), HALF)
    theirs = pl.ds(pl.multiple_of((1 - c) * HALF, 16), HALF)

    def lanes(start, size):
        return pl.ds(pl.multiple_of(start, 128), size)

    def remote(src, dst, s_sem, r_sem, to):
        return pltpu.make_async_remote_copy(src, dst, s_sem, r_sem, device_id=to, device_id_type=MESH)

    sent = []

    def send(src, dst, s_sem, r_sem, to, when=None):
        copy = remote(src, dst, s_sem, r_sem, to)
        if when is None:
            copy.start()
        else:
            pl.when(when)(copy.start)
        sent.append((copy, when))

    def drain():
        for copy, when in sent:
            if when is None:
                copy.wait_send()
            else:
                pl.when(when)(copy.wait_send)
        sent.clear()

    def arrived(ref, sem, when=None):
        copy = remote(ref, ref, sem, sem, sibling)
        if when is None:
            copy.wait_recv()
        else:
            pl.when(when)(copy.wait_recv)

    anc_copy = pltpu.make_async_copy(anc_hbm, anc_ref, anc_sem)
    anc_copy.start()
    kv_local = {}
    for u in (0, 3):
        i = UNITS[u][1]
        for n, ref in enumerate((k_ref, v_ref)):
            copy = pltpu.make_async_copy(
                ref.at[:, lanes((r * 2 + i) * HD, HD)], kv[u].at[me[0], n, mine], kv_l.at[i, n])
            copy.start()
            kv_local[u, n] = copy
    q_local = pltpu.make_async_copy(q_ref.at[:, lanes(r * 2048, 2048)], q_s.at[0, mine], q_l.at[0])
    q_local.start()

    barrier = pltpu.get_barrier_semaphore()
    others = []
    for i in (1, 3):
        there = dev(0, rows[0], col_at(0, i))[0]
        others += [(there, t), (there, x * 2 + 1 - c)]
    others += [dev(0, lax.rem(rows[0] + d, 4), cols[0]) for d in (2, 1, 3)] + [*across, sibling]
    for partner in others:
        pl.semaphore_signal(barrier, inc=1, device_id=partner, device_id_type=MESH)
    pl.semaphore_wait(barrier, len(others))

    def share(u):
        b, i = UNITS[u]
        for n, ref in enumerate((k_ref, v_ref)):
            if b == 0:
                rr = x % 2 * 2 + 1 - c
                send(ref.at[:, lanes((rr * 2 + i) * HD, HD)], kv[u].at[me[0], n, mine],
                     kv_s.at[u, n, 0], kv_r.at[u, n, 0], sibling)
            else:
                for cc in range(2):
                    rr = px % 2 * 2 + cc
                    send(ref.at[:, lanes((rr * 2 + i) * HD, HD)], kv[u].at[me[0], n, mine],
                         kv_s.at[u, n, cc], kv_r.at[u, n, c], across[cc])

    def share_queries():
        for cc in range(2):
            rr = px % 2 * 2 + cc
            send(q_ref.at[:, lanes(rr * 2048, 2048)], q_s.at[1, mine], q_t.at[cc], q_r.at[c], across[cc])
        rr = x % 2 * 2 + 1 - c
        send(q_ref.at[:, lanes(rr * 2048, 2048)], q_s.at[0, mine], q_t.at[2], q_r.at[2], sibling)

    def needed(b, skipped):
        skip = cols[b] == skipped[0]
        for col in skipped[1:]:
            skip = skip | (cols[b] == col)
        return jnp.logical_not((rows[b] == 3) & skip)

    def send_raw():
        for n, to in ((0, 1), (1, 3)):
            there = dev(0, rows[0], col_at(0, to))[0]
            for cc in range(2):
                rr = x % 2 * 2 + cc
                for m, ref in enumerate((k_ref, v_ref)):
                    send(ref.at[:, lanes(rr * 2 * HD, HD)], kv[0].at[me[0], m, mine],
                         zd_s.at[n, cc, m], zd_r.at[n, m, c], (there, x * 2 + cc),
                         needed(0, (3,)) if n == 0 else None)

    def own_ready(u):
        b, i = UNITS[u]
        for n in range(2):
            if b == 0:
                kv_local[u, n].wait()
                arrived(kv[u].at[me[0], n, theirs], kv_r.at[u, n, 0])
            else:
                for cc in range(2):
                    arrived(kv[u].at[me[1], n, pl.ds(cc * HALF, HALF)], kv_r.at[u, n, cc])

    def y_send(u, i):
        b = UNITS[u][0]
        block = kv[u].at[rows[b] * 4 + col_at(b, i)]
        for d in (1, 2, 3):
            send(block, block, ys.at[u, i, d - 1], yr.at[u, rows[b] * 4 + col_at(b, i)],
                 dev(b, lax.rem(rows[b] + d, 4), cols[b]), rows[b] + d < 4)

    def send_own(u, when=None):
        b = UNITS[u][0]
        block = kv[u].at[me[b]]
        kept = needed(b, (3,))
        send(block, block, zs.at[u, 0], zr.at[u, 0], dev(b, rows[b], col_at(b, 1)),
             kept if when is None else when & kept)
        send(block, block, zs.at[u, 1], zr.at[u, 1], dev(b, rows[b], col_at(b, 3)), when)

    def z_near(u):
        b = UNITS[u][0]
        for n, i, to in ((0, 3, 1), (1, 1, 3)):
            block = kv[u].at[rows[b] * 4 + col_at(b, i)]
            if u == 0:
                for m in range(2):
                    for cc in range(2):
                        arrived(block.at[m, pl.ds(cc * HALF, HALF)], zd_r.at[n, m, cc],
                                needed(b, (0,)) if n == 0 else None)
            else:
                arrived(block, zr.at[u, n], needed(b, (0,)) if n == 0 else None)
            y_send(u, i)
            if u:
                pass_half(u, n, i, to)

    def pass_half(u, n, i, to):
        b = UNITS[u][0]
        block = kv[u].at[rows[b] * 4 + col_at(b, i), n]
        send(block, block, zf.at[u, n], zo.at[u, n], dev(b, rows[b], col_at(b, to)),
             needed(b, (0, 3)) if n == 0 else None)

    def z_pass(u):
        for n, i, to in ((0, 3, 1), (1, 1, 3)):
            pass_half(u, n, i, to)

    def z_far(u):
        b = UNITS[u][0]
        block = kv[u].at[rows[b] * 4 + col_at(b, 2)]
        for n in range(2):
            arrived(block.at[n], zo.at[u, n], needed(b, (0, 1)) if n == 0 else None)
        y_send(u, 2)

    def rest(u):
        b = UNITS[u][0]
        for row in range(3):
            for i in (0, 3, 1, 2):
                slot = row * 4 + col_at(b, i)
                arrived(kv[u].at[slot], yr.at[u, slot], rows[b] > row)

    places, listed = [], []

    def read_ancestors():
        anc_copy.wait()
        listed.extend([[anc_ref[x if b == 0 else px, i] for i in range(ANC)] for b in range(2)])
        for b in range(2):
            found = []
            for a in listed[b]:
                a0 = jnp.maximum(a, 0)
                ay, aw = a0 >> 6, (a0 >> 4) & 3
                ay = ay + fam[b] * (3 - 2 * ay)
                aw = aw + fam[b] * (3 - 2 * aw)
                found.append(jnp.where(a >= 0, ay * 4 + aw, me[b]))
            places.append(found + [me[b]])

    def build_bias():
        at_row = lax.broadcasted_iota(jnp.int32, (NODE, KEYS), 0)
        at = lax.broadcasted_iota(jnp.int32, (NODE, KEYS), 1)
        causal = jnp.where(at - ANC * NODE > at_row, -1e30, 0.0)
        for b in range(2):
            bias = causal
            for i, a in enumerate(listed[b]):
                inside = (at >= NODE * i) & (at < NODE * (i + 1))
                bias = jnp.where(inside, jnp.where(a >= 0, 0.0, -1e30), bias)
            bias_s[b] = bias

    def outputs(u):
        b, i = UNITS[u]
        there = out_ref.at[:, lanes((r * 2 + i) * GROUP * HD, GROUP * HD)]
        if b == 0:
            return (remote(o_s.at[u, theirs], there, o_t.at[u, 0], o_r.at[2, i], sibling),
                    pltpu.make_async_copy(o_s.at[u, mine], there, o_l.at[i]))
        return [remote(o_s.at[u, pl.ds(cc * HALF, HALF)], there, o_t.at[u, cc], o_r.at[c, i], across[cc])
                for cc in range(2)]

    def attend(u):
        b, i = UNITS[u]
        keys = jnp.concatenate([kv[u][s, 0] for s in places[b]], axis=0)
        values = jnp.concatenate([kv[u][s, 1] for s in places[b]], axis=0)
        for first in range(0, GROUP, JOINT):
            at = [(i * GROUP + first + j) * HD for j in range(JOINT)]
            queries = jnp.concatenate([q_s[b, :, a:a + HD] for a in at], axis=0)
            scores = lax.dot_general(queries, keys, (((1,), (1,)), ((), ())), preferred_element_type=jnp.float32)
            scores = (scores.reshape(JOINT, NODE, KEYS) + bias_s[b][None]).reshape(JOINT * NODE, KEYS)
            top = jnp.max(scores, axis=-1, keepdims=True)
            weights = jnp.exp2((scores - top) * EXP_SCALE)
            total = jnp.sum(weights, axis=-1, keepdims=True)
            mixed = jnp.dot(weights.astype(jnp.bfloat16), values, preferred_element_type=jnp.float32)
            mixed = (mixed / total).astype(jnp.bfloat16)
            for j in range(JOINT):
                o_s[u, :, (first + j) * HD:(first + j + 1) * HD] = mixed[j * NODE:(j + 1) * NODE]
        for copy in outputs(u):
            copy.start()

    first = (g == 0) & (w > 0)
    send_raw()
    share(0)
    share(1)
    share(2)
    share(3)
    share_queries()
    own_ready(0)
    y_send(0, 0)
    own_ready(1)
    send_own(1)
    y_send(1, 0)
    own_ready(2)
    send_own(2, first)
    own_ready(3)
    send_own(3, first)
    read_ancestors()
    build_bias()
    z_near(0)
    send_own(2, jnp.logical_not(first))
    y_send(2, 0)
    z_near(1)
    send_own(3, jnp.logical_not(first))
    y_send(3, 0)
    z_near(2)
    z_far(1)
    z_pass(0)
    z_near(3)
    z_far(2)
    for cc in range(2):
        arrived(q_s.at[1, pl.ds(cc * HALF, HALF)], q_r.at[cc])
    rest(1)
    attend(1)
    z_far(0)
    q_local.wait()
    arrived(q_s.at[0, theirs], q_r.at[2])
    pl.when(rows[0] == 0)(lambda: attend(0))
    rest(2)
    attend(2)
    z_far(3)
    rest(0)
    pl.when(rows[0] > 0)(lambda: attend(0))
    drain()
    rest(3)
    attend(3)
    drain()
    for u in range(4):
        first_copy, second_copy = outputs(u)
        first_copy.wait_send()
        if UNITS[u][0] == 0:
            second_copy.wait()
        else:
            second_copy.wait_send()
    for i in range(2):
        for n in range(3):
            arrived(out_ref.at[:, pl.ds(0, GROUP * HD)], o_r.at[n, i])


def local(queries, keys, values, ancestors):
    kv = pltpu.VMEM((16, 2, NODE, HD), jnp.bfloat16)
    dma = pltpu.SemaphoreType.DMA
    anywhere = pl.BlockSpec(memory_space=pl.ANY)
    return pl.pallas_call(
        kernel,
        out_shape=pltpu.VMEM((HALF, 8192), jnp.bfloat16),
        in_specs=[anywhere] * 4,
        out_specs=anywhere,
        scratch_shapes=[
            pltpu.SMEM((4, ANC), jnp.int32), dma(()),
            kv, kv, kv, kv,
            pltpu.VMEM((2, NODE, 2048), jnp.bfloat16),
            pltpu.VMEM((4, NODE, 1024), jnp.bfloat16),
            pltpu.VMEM((2, NODE, KEYS), jnp.float32),
            dma((2, 2)), dma((4, 2, 2)), dma((4, 2, 2)), dma((1,)), dma((3,)), dma((3,)),
            dma((4, 2)), dma((4, 2)), dma((4, 2)), dma((4, 2)), dma((2, 2, 2)), dma((2, 2, 2)),
            dma((4, 4, 3)), dma((4, 16)),
            dma((2,)), dma((4, 2)), dma((3, 2)),
        ],
        compiler_params=pltpu.CompilerParams(
            collective_id=0, has_side_effects=True, vmem_limit_bytes=62 << 20),
        cost_estimate=pl.CostEstimate(
            flops=2 * 2 * 96 * 32 * 672 * 128, bytes_accessed=4 << 20, transcendentals=96 * 32 * 672),
        name="tree_attention",
    )(queries, keys, values, ancestors)


def solution(mesh):
    split = P(("dp", "tensor"), None)
    return jax.shard_map(
        local, mesh=mesh, in_specs=(split, split, split, P("dp", None)), out_specs=split, check_vma=False)
```
